1024 devices in a mesh: mem: 64 (over y, x, core), reg: 16 (over z).
Axes of the slice: x: 4, y: 8, z: 16, core: 2. Of those that a mesh axis runs over, the one named last changes fastest.
Arguments:
- ens_state: bfloat16 [1024, 524288], P('mem', 'reg'), may hold values from -6 to 6
- ens_obs: bfloat16 [1024, 262144], P('mem', 'reg'), may hold values from -6 to 6
- innov: bfloat16 [1024, 262144], P('mem', 'reg'), may hold values from -6 to 6
- state_coord: int32 [2, 524288], P(None, 'reg'), may hold values from 0 to 63
- obs_coord: int32 [2, 262144], replicated, may hold values from 0 to 63
- obs_routes: int32 [2048, 1], replicated, may hold values from 0 to 15; in each aligned block of 128 rows (0 to 127, 128 to 255, ...) at most 16 rows name the same one
Outputs:
- analysis: bfloat16 [1024, 524288], P('mem', 'reg')
The draws below stay inside these ranges and needn't reach their ends.
Inputs may be any that keep to these rules, and one draw needn't show every extreme that they name: `obs_routes`: in each aligned block of 128 rows (the observation blocks of one source region) no region is named by more than 16 rows, a bound that some block reaches.
All inputs are finite; a program needn't handle non-finite values.
Results may differ from the reference program's by a relative error of at most 0.0022.
The reference program's roundings to bfloat16 on the way (of `state_anom`, `obs_anom`, `tiles` and `increments`) count: a program that leaves them out, or rounds other values in their place, can miss the bound.
Values may be sent and summed in bfloat16 or wider, within the bound.
A program may use at most 32 MiB of HBM per device.

```python
import math
import jax
import jax.numpy as jnp
import numpy as np
from jax import lax

BLK = 128
SB_DEV = 4
LOC = 32
REGIONS = 16
BANDS = 64
MEMBERS = 1024
STATE_REG = 32768
STATE = 524288
SLOTS = 4
OBK_REG = 128
NOBK = 2048
NOBS = 262144
CAP = 16
N_REG = 16


def ensemble_draw(key, columns):
    key_mean = jax.random.fold_in(key, 0)
    key_spread = jax.random.fold_in(key, 2)
    center = jax.random.uniform(key_mean, (1, columns), jnp.float32, -1.5, 1.5)
    spread = jnp.clip(jax.random.normal(key_spread, (MEMBERS, columns), jnp.float32), -4.0, 4.0)
    return jnp.clip(center + spread, -6.0, 6.0).astype(jnp.bfloat16)


def draw_ens_state(key, part):
    return ensemble_draw(jax.random.fold_in(key, 11), STATE)


def draw_ens_obs(key, part):
    return ensemble_draw(jax.random.fold_in(key, 23), NOBS)


def place_ends(entries, own_key, smallest, high):
    longest = entries.shape.index(max(entries.shape))
    spots = []
    for shift in (0, 1):
        where = [jax.random.randint(jax.random.fold_in(own_key, axis), (), 0, length) for axis, length in enumerate(entries.shape)]
        where[longest] = (where[longest] + shift) % entries.shape[longest]
        spots.append(tuple(where))
    return entries.at[spots[0]].set(smallest).at[spots[1]].set(high)


def shard_levels(rng, dims, cuts, least, largest):
    factor_of, own = 1.0, jax.random.fold_in(rng, 6)
    for axis_at, shards_of in cuts:
        heights = jnp.exp(jax.random.uniform(jax.random.fold_in(own, axis_at), (shards_of,), jnp.float32, least / len(cuts), largest / len(cuts)))
        factor_of = factor_of * jnp.repeat(heights, dims[axis_at] // shards_of).reshape([-1 if axis == axis_at else 1 for axis in range(len(dims))])
    return factor_of


def assign_block(rng, own, number, rows, number_of, top, bound, lean):
    sequence = jax.random.permutation(rng, number_of)
    crowded, common = load_shares(number_of, rows * top, bound, lean, True), load_shares(number_of, rows * top, bound, lean, False)
    places = jnp.arange(number_of)

    def named(lengths, offset_by):
        used = int((lengths > 0).sum())
        fixed = max(1, used // 4)
        moved = fixed + (places - fixed + offset_by * (used - fixed)) % max(1, number_of - fixed)
        return jnp.zeros((number_of,), jnp.int32).at[sequence[jnp.where(places < fixed, places, moved)]].set(jnp.asarray(lengths, jnp.int32))

    lengths = jnp.where(number % 4 == 0, named(crowded, number // 4), named(common, number - number // 4 - 1))
    mixed = jax.random.permutation(jax.random.fold_in(own, 3), number_of)
    giver, sink = mixed[0:number_of // 2 * 2:2], mixed[1:number_of // 2 * 2:2]
    room = jnp.minimum(lengths[giver] - 1, bound - lengths[sink]) // 2
    room = jnp.where((giver == sequence[0]) | (sink == sequence[0]) | (lengths[sink] == 0), 0, jnp.maximum(room, 0))
    moved = jax.random.randint(jax.random.fold_in(own, 4), (number_of // 2,), 0, 1 << 20) % (room + 1)
    lengths = lengths.at[giver].add(-moved).at[sink].add(moved)
    labels = jnp.searchsorted(jnp.cumsum(lengths), jnp.arange(rows * top), side="right").astype(jnp.int32)
    listing = labels.reshape(top, rows).T
    listing = listing[jax.random.permutation(jax.random.fold_in(own, 1), rows)]
    offset_by = jax.random.randint(jax.random.fold_in(own, 2), (rows, 1), 0, top)
    return jnp.take_along_axis(listing, (jnp.arange(top)[None, :] + offset_by) % top, axis=1)


def load_shares(number_of, total, bound, slope, full):
    weights = [(1 << 20) // math.isqrt(rank ** slope) + 1 for rank in range(1, number_of + 1)]
    largest = bound if full else min(bound, max(-(-total // number_of), total * weights[0] // sum(weights)))
    least = 1 if total - largest >= number_of - 1 else 0
    holding, rest = [largest] + [least] * (number_of - 1), total - largest - least * (number_of - 1)
    while rest > 0:
        free = [i for i in range(1, number_of) if holding[i] < largest] or [i for i in range(1, number_of) if holding[i] < bound]
        whole, remaining = sum([weights[i] for i in free]), rest
        for i in free:
            more = min(bound - holding[i], max(1, remaining * weights[i] // whole), rest)
            holding[i] = holding[i] + more
            rest = rest - more
    return np.array(holding)


def normal_values(rng, extent, width, most, pieces=(), held_as=jnp.bfloat16):
    factor_of = shard_levels(rng, extent, pieces, -0.22, 0.18) if pieces else 1.0
    values = jax.random.normal(rng, extent, jnp.float32) * width * factor_of
    return jnp.minimum(jnp.maximum(values, -most), most).astype(held_as)


def setup_inputs(seed: int = 0) -> dict:
    key_list = jax.random.split(jax.random.key(seed), 7)
    ens_state = draw_ens_state(jax.random.fold_in(key_list[6], 71), 0)
    ens_obs = draw_ens_obs(jax.random.fold_in(key_list[6], 71), 0)
    innov = normal_values(key_list[2], (MEMBERS, NOBS), 1.0, 6.0, ((0, 64), (1, 16)))
    state_coord = place_ends(jax.random.randint(key_list[3], (2, STATE), 0, 2 * LOC), jax.random.fold_in(key_list[3], 1), 0, (2 * LOC) - 1).astype(jnp.int32)
    obs_coord = place_ends(jax.random.randint(key_list[4], (2, NOBS), 0, 2 * LOC), jax.random.fold_in(key_list[4], 1), 0, (2 * LOC) - 1).astype(jnp.int32)
    obs_routes_keys = jax.random.split(jax.random.fold_in(key_list[5], 1), NOBK // OBK_REG)
    obs_routes_turns = jax.random.permutation(jax.random.fold_in(key_list[5], 3), NOBK // OBK_REG)
    obs_routes = jax.vmap(lambda own, number: assign_block(jax.random.fold_in(key_list[5], 2), own, number, OBK_REG, N_REG, 1, CAP, 2))(obs_routes_keys, obs_routes_turns).reshape((NOBK, 1))
    return dict(ens_state=ens_state, ens_obs=ens_obs, innov=innov, state_coord=state_coord, obs_coord=obs_coord, obs_routes=obs_routes)


def slot_table(routes, regions, per_region, capacity):
    target = routes[:, 0].reshape(regions, per_region)
    hits = (target[:, :, None] == jnp.arange(regions, dtype=jnp.int32)[None, None, :]).astype(jnp.int32)
    order = jnp.cumsum(hits, axis=1) - 1
    chosen = hits[:, :, :, None] * (order[:, :, :, None] == jnp.arange(capacity, dtype=jnp.int32)[None, None, None, :]).astype(jnp.int32)
    listed = lax.optimization_barrier(jnp.sum(chosen * jnp.arange(per_region, dtype=jnp.int32)[None, :, None, None], axis=1))
    filled = lax.optimization_barrier(jnp.sum(chosen, axis=1))
    return (listed, filled)

def taper_weight(dist_sq):
    ratio = jnp.sqrt(dist_sq) / LOC
    clipped = jnp.maximum(ratio, 1.0)
    inner = (((-0.25 * ratio + 0.5) * ratio + 0.625) * ratio - 5.0 / 3.0) * ratio * ratio + 1.0
    outer = ((((ratio / 12.0 - 0.5) * ratio + 0.625) * ratio + 5.0 / 3.0) * ratio - 5.0) * ratio + 4.0 - 2.0 / (3.0 * clipped)
    return jnp.where(ratio <= 1.0, inner, jnp.where(ratio < 2.0, outer, 0.0))

def reference(ens_state, ens_obs, innov, state_coord, obs_coord, obs_routes):
    members = ens_state.shape[0]
    state_wide = ens_state.astype(jnp.float32)
    state_anom = (state_wide - lax.optimization_barrier(jnp.mean(state_wide, axis=0, keepdims=True))).astype(jnp.bfloat16)
    obs_wide = ens_obs.astype(jnp.float32)
    obs_anom = (obs_wide - lax.optimization_barrier(jnp.mean(obs_wide, axis=0, keepdims=True))).astype(jnp.bfloat16)
    listed, filled = slot_table(obs_routes, REGIONS, OBK_REG, CAP)
    obs_blocks = obs_anom.reshape(members, NOBK, BLK)
    innov_blocks = innov.reshape(members, NOBK, BLK)
    coord_blocks = obs_coord.reshape(2, NOBK, BLK)
    source = jnp.arange(REGIONS * CAP, dtype=jnp.int32) // CAP
    column = jnp.arange(REGIONS * CAP, dtype=jnp.int32) % CAP
    band_rows = SB_DEV * BLK

    def region(index):
        local = listed[source, index, column]
        present = filled[source, index, column].astype(jnp.bfloat16)
        block_ids = (source * OBK_REG + local).astype(jnp.int32)
        picked = jnp.take(obs_blocks, block_ids, axis=1) * present[None, :, None]
        weights = jnp.take(innov_blocks, block_ids, axis=1) * present[None, :, None]
        obs_xy = jnp.take(coord_blocks, block_ids, axis=1).reshape(2, BANDS, SLOTS * BLK)
        start = (index * STATE_REG).astype(jnp.int32)
        rows = lax.dynamic_slice_in_dim(state_anom, start, STATE_REG, 1)
        rows_xy = lax.dynamic_slice_in_dim(state_coord, start, STATE_REG, 1).reshape(2, BANDS, band_rows)
        rows_band = rows.reshape(members, BANDS, band_rows).astype(jnp.float32)
        picked_band = picked.reshape(members, BANDS, SLOTS * BLK).astype(jnp.float32)
        cov = jnp.einsum('jbi,jbq->biq', rows_band, picked_band) / (members - 1)
        delta_x = rows_xy[0][:, :, None] - obs_xy[0][:, None, :]
        delta_y = rows_xy[1][:, :, None] - obs_xy[1][:, None, :]
        dist_sq = (delta_x * delta_x + delta_y * delta_y).astype(jnp.float32)
        tiles = (cov * taper_weight(dist_sq)).astype(jnp.bfloat16)
        weights_band = weights.reshape(members, BANDS, SLOTS * BLK).astype(jnp.float32)
        increments = jnp.einsum('jbq,biq->jbi', weights_band, tiles.astype(jnp.float32))
        return increments.astype(jnp.bfloat16).reshape(members, STATE_REG)
    per_region = lax.map(region, jnp.arange(REGIONS, dtype=jnp.int32))
    increments = jnp.transpose(per_region, (1, 0, 2)).reshape(members, STATE)
    return (state_wide + increments.astype(jnp.float32)).astype(jnp.bfloat16)
```

```python
import jax
import jax.numpy as jnp
from jax import lax
from jax.sharding import PartitionSpec as P

BLK = 128
LOC = 32
SLOTS = 4


def slots_of(target, wanted):
    k = jnp.arange(target.shape[0], dtype=jnp.int32)
    earlier = (target[None, :] == target[:, None]) & (k[None, :] < k[:, None])
    rank = jnp.sum(earlier.astype(jnp.int32), axis=1)
    return (target[None, :] == wanted[0][:, None]) & (rank[None, :] == wanted[1][:, None])


def taper_weight(dist_sq):
    ratio = jnp.sqrt(dist_sq) / LOC
    clipped = jnp.maximum(ratio, 1.0)
    inner = (((-0.25 * ratio + 0.5) * ratio + 0.625) * ratio - 5.0 / 3.0) * ratio * ratio + 1.0
    outer = (
        ((((ratio / 12.0 - 0.5) * ratio + 0.625) * ratio + 5.0 / 3.0) * ratio - 5.0) * ratio
        + 4.0
        - 2.0 / (3.0 * clipped)
    )
    return jnp.where(ratio <= 1.0, inner, jnp.where(ratio < 2.0, outer, 0.0))


def anomaly(rows):
    wide = rows.astype(jnp.float32)
    return (wide - jnp.mean(wide, axis=0, keepdims=True)).astype(jnp.bfloat16)


def per_device(ens_state, ens_obs, innov, state_coord, obs_coord, obs_routes):
    regions = lax.axis_size("reg")
    bands = lax.axis_size("mem")
    region_idx = lax.axis_index("reg")
    band_idx = lax.axis_index("mem")
    mem_dev = ens_state.shape[0]
    members = mem_dev * bands
    per_region = ens_obs.shape[1] // BLK
    capacity = SLOTS * bands // regions
    wide = SLOTS * BLK
    state_rows = lax.all_to_all(ens_state, "mem", split_axis=1, concat_axis=0, tiled=True)
    routes = obs_routes[:, 0]
    target = lax.dynamic_slice_in_dim(routes, region_idx * per_region, per_region)
    q = jnp.arange(regions * capacity, dtype=jnp.int32)
    hot = slots_of(target, (q // capacity, q % capacity)).astype(jnp.bfloat16)
    both = jnp.stack([ens_obs, innov]).reshape(2, mem_dev, per_region, BLK)
    pick = jnp.einsum(
        "gsk,amkx->gamsx",
        hot.reshape(bands, SLOTS, per_region),
        both,
        preferred_element_type=jnp.float32,
    ).astype(jnp.bfloat16)
    pick = pick.reshape(regions, bands // regions * 2 * mem_dev, wide)
    recv = lax.all_to_all(pick, "reg", split_axis=0, concat_axis=0, tiled=True)
    recv = recv.reshape(bands, 2 * mem_dev, wide)
    rows = lax.all_to_all(recv, "mem", split_axis=0, concat_axis=0, tiled=True)
    rows = rows.reshape(bands, 2, mem_dev, wide)
    obs_rows = rows[:, 0].reshape(members, wide)
    innov_rows = rows[:, 1].reshape(members, wide)
    band_rows = state_rows.shape[1]
    rows_xy = lax.dynamic_slice_in_dim(state_coord, band_idx * band_rows, band_rows, 1)
    slot_ids = band_idx * SLOTS + jnp.arange(SLOTS, dtype=jnp.int32)
    source = band_idx * SLOTS // capacity
    theirs = lax.dynamic_slice_in_dim(routes, source * per_region, per_region)
    here = slots_of(theirs, (jnp.full((SLOTS,), region_idx), slot_ids % capacity)).astype(jnp.int32)
    filled = jnp.sum(here, axis=1)
    block_ids = source * per_region + jnp.sum(here * jnp.arange(per_region, dtype=jnp.int32), axis=1)
    obs_xy = jnp.concatenate(
        [lax.dynamic_slice_in_dim(obs_coord, block_ids[s] * BLK, BLK, 1) for s in range(SLOTS)], axis=1
    )
    cov = lax.dot_general(
        anomaly(state_rows), anomaly(obs_rows), (((0,), (0,)), ((), ())), preferred_element_type=jnp.float32
    ) / (members - 1)
    delta_x = rows_xy[0][:, None] - obs_xy[0][None, :]
    delta_y = rows_xy[1][:, None] - obs_xy[1][None, :]
    dist_sq = (delta_x * delta_x + delta_y * delta_y).astype(jnp.float32)
    present = jnp.repeat(filled, BLK).astype(jnp.float32)
    tiles = (cov * (taper_weight(dist_sq) * present[None, :])).astype(jnp.bfloat16)
    increments = lax.dot_general(
        innov_rows, tiles, (((1,), (1,)), ((), ())), preferred_element_type=jnp.float32
    ).astype(jnp.bfloat16)
    returned = lax.all_to_all(increments, "mem", split_axis=0, concat_axis=1, tiled=True)
    return (ens_state.astype(jnp.float32) + returned.astype(jnp.float32)).astype(jnp.bfloat16)


def solution(mesh):
    return jax.shard_map(
        per_device,
        mesh=mesh,
        in_specs=(P("mem", "reg"), P("mem", "reg"), P("mem", "reg"), P(None, "reg"), P(), P()),
        out_specs=P("mem", "reg"),
        check_vma=False,
    )
```

```python
import functools

import jax
import jax.numpy as jnp
from jax import lax
from jax.experimental import pallas as pl
from jax.experimental.pallas import tpu as pltpu
from jax.sharding import PartitionSpec as P

BLK = 128
LOC = 32
SLOTS = 4
WINDOW = 5
LAG = 4
PREP = 9
MESH = pl.DeviceIdType.MESH


def slots_of(target, region, rank):
    k = jnp.arange(target.shape[0], dtype=jnp.int32)
    earlier = (target[None, :] == target[:, None]) & (k[None, :] < k[:, None])
    order = jnp.sum(earlier.astype(jnp.int32), axis=1)
    return ((target[None, :] == region[:, None]) & (order[None, :] == rank[:, None])).astype(jnp.int32)


def taper_weight(dist_sq):
    ratio = jnp.sqrt(dist_sq) / LOC
    clipped = jnp.maximum(ratio, 1.0)
    inner = (((-0.25 * ratio + 0.5) * ratio + 0.625) * ratio - 5.0 / 3.0) * ratio * ratio + 1.0
    outer = (
        ((((ratio / 12.0 - 0.5) * ratio + 0.625) * ratio + 5.0 / 3.0) * ratio - 5.0) * ratio
        + 4.0
        - 2.0 / (3.0 * clipped)
    )
    return jnp.where(ratio <= 1.0, inner, jnp.where(ratio < 2.0, outer, 0.0))


def anomaly(rows):
    wide = rows.astype(jnp.float32)
    return (wide - jnp.mean(wide, axis=0, keepdims=True)).astype(jnp.bfloat16)


def place_of(source, group, groups):
    return lax.div(source, 2) * (2 * groups) + 2 * group + lax.rem(source, 2)


def band_of(place, groups):
    source = 2 * lax.div(place, 2 * groups) + lax.rem(place, 2)
    return source, lax.div(lax.rem(place, 2 * groups), 2)


def loop(start, stop, body):
    def step(i, carry):
        body(i)
        return carry

    lax.fori_loop(start, stop, step, 0)


def gather(n_reg, ids, obs, innov, pack):
    region = lax.axis_index("reg")
    groups = pack.shape[1]

    @functools.partial(loop, 0, n_reg)
    def _(shift):
        to = lax.rem(region + shift, n_reg)
        for c in range(groups * SLOTS):
            lanes = pl.ds(pl.multiple_of(ids[to * (groups * SLOTS) + c] * BLK, BLK), BLK)
            at = pl.ds(c % SLOTS * BLK, BLK)
            pack[shift, c // SLOTS, 0, :, at] = obs[:, lanes]
            pack[shift, c // SLOTS, 1, :, at] = innov[:, lanes]


def kernel(
    n_mem, n_reg, state, pack, rows_xy, obs_xy, present, returned, land,
    rows, rows_t, pair, taper, tiles, incr,
    z_send, z_recv, s_send, s_recv, f_send, f_recv, r_send, r_recv,
):
    mine, region = lax.axis_index("mem"), lax.axis_index("reg")
    groups = n_mem // n_reg
    my_source, my_group = band_of(mine, groups)
    per = state.shape[0]
    members, wide = rows.shape
    my_rows = pl.ds(pl.multiple_of(mine * per, per), per)

    def columns(band):
        return pl.ds(pl.multiple_of(band * wide, wide), wide)

    def remote(src, dst, send, recv, mem, reg):
        return pltpu.make_async_remote_copy(
            src_ref=src, dst_ref=dst, send_sem=send, recv_sem=recv, device_id=(mem, reg), device_id_type=MESH
        )

    barrier = pltpu.get_barrier_semaphore()

    @functools.partial(loop, 1, n_mem)
    def _(s):
        pl.semaphore_signal(barrier, inc=1, device_id=(lax.rem(mine + s, n_mem), region), device_id_type=MESH)

    @functools.partial(loop, 1, n_reg)
    def _(s):
        pl.semaphore_signal(barrier, inc=1, device_id=(mine, lax.rem(region + s, n_reg)), device_id_type=MESH)

    def shift_of(k):
        half = lax.div(k + 1, 2)
        return half + (1 - lax.rem(k, 2)) * (n_reg - 2 * half) * jnp.minimum(k, 1)

    def along_z(shift, group):
        return remote(
            pack.at[shift, group], land.at[shift, group], z_send.at[shift, group], z_recv.at[shift, group],
            mine, lax.rem(region + shift, n_reg),
        )

    def send_z(k):
        shift = shift_of(k)
        for group in range(groups):
            along_z(shift, group).start()

    pl.semaphore_wait(barrier, n_mem + n_reg - 2)
    loop(1, min(WINDOW, n_reg - 1) + 1, send_z)

    @functools.partial(loop, 1, n_mem)
    def _(s):
        to = lax.rem(mine + s, n_mem)
        source, group = band_of(to, groups)
        remote(state.at[:, columns(source * groups + group)], rows.at[my_rows], s_send, s_recv, to, region).start()

    pltpu.make_async_copy(state.at[:, columns(my_source * groups + my_group)], rows.at[my_rows], s_recv).start()

    def make_taper(i):
        at = pl.ds(pl.multiple_of(i * BLK, BLK), BLK)
        dx = rows_xy[at, 0:1] - obs_xy[0:1, :]
        dy = rows_xy[at, 1:2] - obs_xy[1:2, :]
        near = taper_weight((dx * dx + dy * dy).astype(jnp.float32))
        taper[at, :] = near * (present[0:1, :] / (members - 1))

    loop(0, wide // BLK, make_taper)

    def forward(shift, held):
        source = lax.rem(region + n_reg - shift, n_reg)
        for group in range(groups):
            to = place_of(source, group, groups)

            if held is land:
                along_z(shift, group).wait_recv()

            @pl.when(to != mine)
            def _():
                remote(held.at[shift, group], pair.at[:, my_rows], f_send, f_recv, to, region).start()

            @pl.when(to == mine)
            def _():
                pltpu.make_async_copy(held.at[shift, group], pair.at[:, my_rows], f_recv).start()

    def prepare():
        pltpu.make_async_copy(rows, rows, s_recv).wait()

        @functools.partial(loop, 0, wide // BLK)
        def _(i):
            at = pl.ds(pl.multiple_of(i * BLK, BLK), BLK)
            rows_t[at, :] = anomaly(rows[:, at]).astype(jnp.float32).T.astype(jnp.bfloat16)

    def update():
        pltpu.make_async_copy(pair, pair, f_recv).wait()
        half = wide // 2

        @functools.partial(loop, 0, 2)
        def _(i):
            at = pl.ds(pl.multiple_of(i * half, half), half)
            cov = jnp.dot(rows_t[...], anomaly(pair[0, :, at]), preferred_element_type=jnp.float32)
            tiles[:, at] = (cov * taper[:, at]).astype(jnp.bfloat16)

        share = n_mem // 4

        @functools.partial(loop, 0, 4)
        def _(i):
            part = lax.rem(lax.div(mine, share) + i, 4)
            at = pl.ds(pl.multiple_of(part * (share * per), share * per), share * per)
            incr[at, :] = lax.dot_general(
                pair[1, at, :], tiles[...], (((1,), (1,)), ((), ())), preferred_element_type=jnp.float32
            ).astype(jnp.bfloat16)

            @functools.partial(loop, 0, share)
            def _(s):
                to = part * share + lax.rem(mine + s, share)
                src = incr.at[pl.ds(pl.multiple_of(to * per, per), per)]
                dst = returned.at[:, columns(my_source * groups + my_group)]

                @pl.when(to != mine)
                def _():
                    remote(src, dst, r_send, r_recv, to, region).start()

                @pl.when(to == mine)
                def _():
                    pltpu.make_async_copy(src, dst, r_recv).start()

    my_shift = lax.rem(region + n_reg - my_source, n_reg)
    ahead = jnp.minimum(my_shift, n_reg - my_shift)
    my_step = 2 * ahead - jnp.where(my_shift == ahead, 1, 0) * jnp.minimum(ahead, 1) + LAG
    prep_step = jnp.minimum(my_step, PREP)

    forward(0, pack)

    @functools.partial(loop, 1, n_reg + LAG)
    def _(k):
        @pl.when(k + WINDOW < n_reg)
        def _():
            send_z(k + WINDOW)

        @pl.when(k < n_reg)
        def _():
            forward(shift_of(k), land)

        pl.when(k == prep_step)(prepare)
        pl.when(k == my_step)(update)

    def drain(k):
        for group in range(groups):
            along_z(shift_of(k), group).wait_send()

    loop(1, n_reg, drain)
    sent = rows.at[pl.ds(0, (n_mem - 1) * per)]
    pltpu.make_async_copy(sent, sent, s_send).wait()
    pltpu.make_async_copy(sent, sent, r_send).wait()
    both = pair.at[:, pl.ds(0, (n_mem - 1) * per)]
    pltpu.make_async_copy(both, both, f_send).wait()
    pltpu.make_async_copy(returned, returned, r_recv).wait()


def per_device(ens_state, ens_obs, innov, state_coord, obs_coord, obs_routes):
    n_reg, n_mem = lax.axis_size("reg"), lax.axis_size("mem")
    region, mine = lax.axis_index("reg"), lax.axis_index("mem")
    per = ens_state.shape[0]
    per_region = ens_obs.shape[1] // BLK
    groups = n_mem // n_reg
    capacity = SLOTS * groups
    wide = ens_state.shape[1] // n_mem
    paired = SLOTS * BLK
    routes = obs_routes[:, 0]
    k = jnp.arange(per_region, dtype=jnp.int32)
    q = jnp.arange(n_reg * capacity, dtype=jnp.int32)
    target = lax.dynamic_slice_in_dim(routes, region * per_region, per_region)
    ids = jnp.sum(slots_of(target, q // capacity, q % capacity) * k, axis=1)
    source, group = band_of(mine, groups)
    theirs = lax.dynamic_slice_in_dim(routes, source * per_region, per_region)
    here = slots_of(
        theirs, jnp.full((SLOTS,), region), group * SLOTS + jnp.arange(SLOTS, dtype=jnp.int32)
    )
    blocks = source * per_region + jnp.sum(here * k, axis=1)
    present = jnp.repeat(jnp.sum(here, axis=1), BLK).astype(jnp.float32)[None, :]
    obs_xy = jnp.concatenate(
        [lax.dynamic_slice_in_dim(obs_coord, blocks[s] * BLK, BLK, 1) for s in range(SLOTS)], axis=1
    )
    rows_xy = lax.dynamic_slice_in_dim(state_coord, (source * groups + group) * wide, wide, 1).T
    members = per * n_mem
    vmem = pl.BlockSpec(memory_space=pltpu.VMEM)
    half = jnp.bfloat16
    smem = pl.BlockSpec(memory_space=pltpu.SMEM)
    anywhere = pl.BlockSpec(memory_space=pl.ANY)
    pack = pl.pallas_call(
        functools.partial(gather, n_reg),
        out_shape=jax.ShapeDtypeStruct((n_reg, groups, 2, per, paired), half),
        in_specs=[smem, vmem, vmem],
        out_specs=vmem,
        compiler_params=pltpu.CompilerParams(vmem_limit_bytes=16 * 2**20),
    )(ids, ens_obs, innov)
    returned = pl.pallas_call(
        functools.partial(kernel, n_mem, n_reg),
        out_shape=jax.ShapeDtypeStruct(ens_state.shape, half),
        in_specs=[anywhere, anywhere, vmem, vmem, vmem],
        out_specs=anywhere,
        scratch_shapes=[
            pltpu.VMEM((n_reg, groups, 2, per, paired), half),
            pltpu.VMEM((members, wide), half),
            pltpu.VMEM((wide, members), half),
            pltpu.VMEM((2, members, paired), half),
            pltpu.VMEM((wide, paired), jnp.float32),
            pltpu.VMEM((wide, paired), half),
            pltpu.VMEM((members, wide), half),
            pltpu.SemaphoreType.DMA((n_reg, groups)),
            pltpu.SemaphoreType.DMA((n_reg, groups)),
        ]
        + [pltpu.SemaphoreType.DMA] * 6,
        compiler_params=pltpu.CompilerParams(
            collective_id=0, has_side_effects=True, vmem_limit_bytes=48 * 2**20
        ),
    )(ens_state, pack, rows_xy, obs_xy, present)
    return (ens_state.astype(jnp.float32) + returned.astype(jnp.float32)).astype(jnp.bfloat16)


def solution(mesh):
    return jax.shard_map(
        per_device,
        mesh=mesh,
        in_specs=(P("mem", "reg"), P("mem", "reg"), P("mem", "reg"), P(None, "reg"), P(), P()),
        out_specs=P("mem", "reg"),
        check_vma=False,
    )
```

```python
import functools

import jax
import jax.numpy as jnp
from jax import lax
from jax.experimental import pallas as pl
from jax.experimental.pallas import tpu as pltpu
from jax.sharding import PartitionSpec as P

BLK = 128
LOC = 32
SLOTS = 4
WINDOW = 20
LAG = 12
PREP = 26
STATES = 3
MESH = pl.DeviceIdType.MESH


def taper_weight(dist_sq):
    ratio = jnp.sqrt(dist_sq) / LOC
    clipped = jnp.maximum(ratio, 1.0)
    inner = (((-0.25 * ratio + 0.5) * ratio + 0.625) * ratio - 5.0 / 3.0) * ratio * ratio + 1.0
    outer = (
        ((((ratio / 12.0 - 0.5) * ratio + 0.625) * ratio + 5.0 / 3.0) * ratio - 5.0) * ratio
        + 4.0
        - 2.0 / (3.0 * clipped)
    )
    return jnp.where(ratio <= 1.0, inner, jnp.where(ratio < 2.0, outer, 0.0))


def anomaly(rows):
    wide = rows.astype(jnp.float32)
    return (wide - jnp.mean(wide, axis=0, keepdims=True)).astype(jnp.bfloat16)


def place_of(source, group, groups):
    y = lax.div(source, 2)
    x = 2 * lax.rem(source, 2) + lax.rem(lax.div(group, 2) + y, 2)
    return y * (2 * groups) + 2 * x + lax.rem(group, 2)


def band_of(place, groups):
    y = lax.div(place, 2 * groups)
    x = lax.div(lax.rem(place, 2 * groups), 2)
    return 2 * y + lax.div(x, 2), 2 * lax.rem(x + y, 2) + lax.rem(place, 2)


def loop(start, stop, body):
    def step(i, carry):
        body(i)
        return carry

    lax.fori_loop(start, stop, step, 0)


def stage(
    n_mem, n_reg, routes, obs, innov, state_xy, obs_xy, pack, rows_at, obs_at, present,
    obs_in, innov_in, ids, counts, mine_ids, sems,
):
    mine, region = lax.axis_index("mem"), lax.axis_index("reg")
    groups, per_region, wide = n_mem // n_reg, routes.shape[1], rows_at.shape[1]
    capacity = groups * SLOTS
    source, group = band_of(mine, groups)
    band = source * groups + group
    copies = [
        pltpu.make_async_copy(obs, obs_in, sems.at[0]),
        pltpu.make_async_copy(innov, innov_in, sems.at[1]),
        pltpu.make_async_copy(
            state_xy.at[:, pl.ds(pl.multiple_of(band * wide, wide), wide)], rows_at, sems.at[2]
        ),
    ]
    for copy in copies:
        copy.start()

    @functools.partial(loop, 0, n_reg)
    def _(r):
        counts[r] = 0
        for c in range(capacity):
            ids[r * capacity + c] = 0

    for s in range(SLOTS):
        mine_ids[s] = 0

    def tally(k, seen):
        to = routes[region, k]
        at = counts[to]
        ids[to * capacity + at] = k
        counts[to] = at + 1
        hit = routes[source, k] == region
        slot = seen - group * SLOTS

        @pl.when(hit & (slot >= 0) & (slot < SLOTS))
        def _():
            mine_ids[slot] = k

        return seen + hit.astype(jnp.int32)

    total = lax.fori_loop(0, per_region, tally, 0)
    for s in range(SLOTS):
        block = source * per_region + mine_ids[s]
        at = pl.ds(s * BLK, BLK)
        copy = pltpu.make_async_copy(
            obs_xy.at[:, pl.ds(pl.multiple_of(block * BLK, BLK), BLK)], obs_at.at[:, at], sems.at[3 + s]
        )
        copy.start()
        copies.append(copy)
        filled = (group * SLOTS + s < total).astype(jnp.int32)
        present[:, at] = jnp.full((1, BLK), filled, jnp.int32).astype(jnp.float32)
    copies[0].wait()
    copies[1].wait()

    @functools.partial(loop, 0, n_reg)
    def _(shift):
        to = lax.rem(region + shift, n_reg)
        for c in range(capacity):
            lanes = pl.ds(pl.multiple_of(ids[to * capacity + c] * BLK, BLK), BLK)
            at = pl.ds(c % SLOTS * BLK, BLK)
            pack[shift, c // SLOTS, 0, :, at] = obs_in[:, lanes]
            pack[shift, c // SLOTS, 1, :, at] = innov_in[:, lanes]

    for copy in copies[2:]:
        copy.wait()


def batched(start, stop, body, most=8):
    size = max(n for n in range(1, most + 1) if (stop - start) % n == 0)

    @functools.partial(loop, 0, (stop - start) // size)
    def _(i):
        for j in range(size):
            body(start + i * size + j)


def kernel(
    n_mem, n_reg, state, pack, rows_xy, obs_xy, present, returned, land,
    rows, rows_t, pair, taper, tiles, incr,
    z_send, z_recv, s_send, s_recv, f_send, f_recv, r_send, r_recv,
):
    mine, region = lax.axis_index("mem"), lax.axis_index("reg")
    groups = n_mem // n_reg
    my_source, my_group = band_of(mine, groups)
    per = state.shape[0]
    members, wide = rows.shape
    my_rows = pl.ds(pl.multiple_of(mine * per, per), per)

    def columns(band):
        return pl.ds(pl.multiple_of(band * wide, wide), wide)

    def remote(src, dst, send, recv, mem, reg):
        return pltpu.make_async_remote_copy(
            src_ref=src, dst_ref=dst, send_sem=send, recv_sem=recv, device_id=(mem, reg), device_id_type=MESH
        )

    barrier = pltpu.get_barrier_semaphore()

    @functools.partial(loop, 1, n_mem)
    def _(s):
        pl.semaphore_signal(barrier, inc=1, device_id=(lax.rem(mine + s, n_mem), region), device_id_type=MESH)

    @functools.partial(loop, 1, n_reg)
    def _(s):
        pl.semaphore_signal(barrier, inc=1, device_id=(mine, lax.rem(region + s, n_reg)), device_id_type=MESH)

    turn = 2 * lax.rem(lax.div(mine, 2), groups) + lax.div(mine, 2 * groups)

    def piece_of(k):
        at = lax.rem(k, n_reg)
        near = lax.rem(lax.div(at, 2) + turn, n_reg // 2)
        other = jnp.where(near == 0, n_reg // 2, n_reg - near)
        return lax.div(k, n_reg), jnp.where(lax.rem(at, 2) == 0, near, other)

    def along_z(group, shift):
        return remote(
            pack.at[shift, group], land.at[shift, group], z_send.at[shift, group], z_recv.at[shift, group],
            mine, lax.rem(region + shift, n_reg),
        )

    def stays(group, shift):
        return pltpu.make_async_copy(pack.at[shift, group], land.at[shift, group], z_recv.at[shift, group])

    def send_z(k):
        group, shift = piece_of(k)

        @pl.when(shift > 0)
        def _():
            along_z(group, shift).start()

        @pl.when(shift == 0)
        def _():
            stays(group, shift).start()

    pl.semaphore_wait(barrier, n_mem + n_reg - 2)
    steps = n_reg * groups
    loop(0, min(WINDOW, steps), send_z)
    pltpu.make_async_copy(state.at[:, columns(my_source * groups + my_group)], rows.at[my_rows], s_recv).start()

    def nth(s):
        half = lax.div(s + 1, 2)
        return lax.rem(mine + jnp.where(lax.rem(s, 2) == 1, half, n_mem - half), n_mem)

    def send_state(s):
        to = nth(s)
        source, group = band_of(to, groups)
        remote(state.at[:, columns(source * groups + group)], rows.at[my_rows], s_send, s_recv, to, region).start()

    def make_taper(i):
        at = pl.ds(pl.multiple_of(i * BLK, BLK), BLK)
        mine_xy = [
            jnp.broadcast_to(rows_xy[a : a + 1, at].astype(jnp.float32), (BLK, BLK)).T[:, 0:1] for a in range(2)
        ]
        dx = mine_xy[0] - obs_xy[0:1, :].astype(jnp.float32)
        dy = mine_xy[1] - obs_xy[1:2, :].astype(jnp.float32)
        taper[at, :] = taper_weight(dx * dx + dy * dy) * (present[0:1, :] / (members - 1))

    loop(0, wide // BLK, make_taper)

    def forward(k):
        group, shift = piece_of(k)
        source = lax.rem(region + n_reg - shift, n_reg)
        to = place_of(source, group, groups)
        stays(group, shift).wait()

        @pl.when(to != mine)
        def _():
            remote(land.at[shift, group], pair.at[:, my_rows], f_send, f_recv, to, region).start()

        @pl.when(to == mine)
        def _():
            pltpu.make_async_copy(land.at[shift, group], pair.at[:, my_rows], f_recv).start()

    def prepare():
        pltpu.make_async_copy(rows, rows, s_recv).wait()

        @functools.partial(loop, 0, wide // BLK)
        def _(i):
            at = pl.ds(pl.multiple_of(i * BLK, BLK), BLK)
            rows_t[at, :] = anomaly(rows[:, at]).astype(jnp.float32).T.astype(jnp.bfloat16)

    def update():
        pltpu.make_async_copy(pair, pair, f_recv).wait()
        half = wide // 2

        @functools.partial(loop, 0, 2)
        def _(i):
            at = pl.ds(pl.multiple_of(i * half, half), half)
            cov = jnp.dot(rows_t[...], anomaly(pair[0, :, at]), preferred_element_type=jnp.float32)
            tiles[:, at] = (cov * taper[:, at]).astype(jnp.bfloat16)

        part = members // 4

        @functools.partial(loop, 0, 4)
        def _(i):
            at = pl.ds(pl.multiple_of(i * part, part), part)
            incr[at, :] = lax.dot_general(
                pair[1, at, :], tiles[...], (((1,), (1,)), ((), ())), preferred_element_type=jnp.float32
            ).astype(jnp.bfloat16)

        dst = returned.at[:, columns(my_source * groups + my_group)]
        pltpu.make_async_copy(incr.at[my_rows], dst, r_recv).start()

        def give(s):
            to = nth(s)
            remote(incr.at[pl.ds(pl.multiple_of(to * per, per), per)], dst, r_send, r_recv, to, region).start()

        batched(1, n_mem, give)

    my_step = (my_group + 1) * n_reg + LAG

    @functools.partial(loop, 0, steps + LAG + 1)
    def _(k):
        @pl.when(k + WINDOW < steps)
        def _():
            send_z(k + WINDOW)

        for i in range(STATES):
            s = STATES * k + i + 1

            @pl.when(s < n_mem)
            def _():
                send_state(s)

        pl.when(k < steps)(lambda: forward(k))
        pl.when(k == jnp.minimum(PREP, my_step))(prepare)
        pl.when(k == my_step)(update)

    @functools.partial(loop, 0, groups)
    def _(group):
        loop(1, n_reg, lambda shift: along_z(group, shift).wait_send())

    sent = rows.at[pl.ds(0, (n_mem - 1) * per)]
    pltpu.make_async_copy(sent, sent, s_send).wait()
    pltpu.make_async_copy(sent, sent, r_send).wait()
    both = pair.at[:, pl.ds(0, (n_mem - 1) * per)]
    pltpu.make_async_copy(both, both, f_send).wait()
    pltpu.make_async_copy(returned, returned, r_recv).wait()


def per_device(ens_state, ens_obs, innov, state_coord, obs_coord, obs_routes):
    n_reg, n_mem = lax.axis_size("reg"), lax.axis_size("mem")
    per = ens_state.shape[0]
    per_region = ens_obs.shape[1] // BLK
    groups = n_mem // n_reg
    capacity = SLOTS * groups
    wide = ens_state.shape[1] // n_mem
    paired = SLOTS * BLK
    members = per * n_mem
    vmem = pl.BlockSpec(memory_space=pltpu.VMEM)
    hbm = pl.BlockSpec(memory_space=pltpu.HBM)
    anywhere = pl.BlockSpec(memory_space=pl.ANY)
    half = jnp.bfloat16
    pack, rows_xy, obs_xy, present = pl.pallas_call(
        functools.partial(stage, n_mem, n_reg),
        out_shape=[
            jax.ShapeDtypeStruct((n_reg, groups, 2, per, paired), half),
            jax.ShapeDtypeStruct((2, wide), jnp.int32),
            jax.ShapeDtypeStruct((2, paired), jnp.int32),
            jax.ShapeDtypeStruct((1, paired), jnp.float32),
        ],
        in_specs=[pl.BlockSpec(memory_space=pltpu.SMEM), hbm, hbm, hbm, hbm],
        out_specs=[vmem] * 4,
        scratch_shapes=[
            pltpu.VMEM(ens_obs.shape, half),
            pltpu.VMEM(innov.shape, half),
            pltpu.SMEM((n_reg * capacity,), jnp.int32),
            pltpu.SMEM((n_reg,), jnp.int32),
            pltpu.SMEM((SLOTS,), jnp.int32),
            pltpu.SemaphoreType.DMA((3 + SLOTS,)),
        ],
        compiler_params=pltpu.CompilerParams(vmem_limit_bytes=58 * 2**20),
    )(obs_routes.reshape(n_reg, per_region), ens_obs, innov, state_coord, obs_coord)
    returned = pl.pallas_call(
        functools.partial(kernel, n_mem, n_reg),
        out_shape=jax.ShapeDtypeStruct(ens_state.shape, half),
        in_specs=[anywhere, anywhere, vmem, vmem, vmem],
        out_specs=anywhere,
        scratch_shapes=[
            pltpu.VMEM((n_reg, groups, 2, per, paired), half),
            pltpu.VMEM((members, wide), half),
            pltpu.VMEM((wide, members), half),
            pltpu.VMEM((2, members, paired), half),
            pltpu.VMEM((wide, paired), jnp.float32),
            pltpu.VMEM((wide, paired), half),
            pltpu.VMEM((members, wide), half),
            pltpu.SemaphoreType.DMA((n_reg, groups)),
            pltpu.SemaphoreType.DMA((n_reg, groups)),
        ]
        + [pltpu.SemaphoreType.DMA] * 6,
        compiler_params=pltpu.CompilerParams(
            collective_id=0, has_side_effects=True, vmem_limit_bytes=58 * 2**20
        ),
    )(ens_state, pack, rows_xy, obs_xy, present)
    return (ens_state.astype(jnp.float32) + returned.astype(jnp.float32)).astype(jnp.bfloat16)


def solution(mesh):
    return jax.shard_map(
        per_device,
        mesh=mesh,
        in_specs=(P("mem", "reg"), P("mem", "reg"), P("mem", "reg"), P(None, "reg"), P(), P()),
        out_specs=P("mem", "reg"),
        check_vma=False,
    )
```
